1024 devices in a mesh: section: 4 (over x), expert: 32 (over z, y_lo), dp: 8 (over y_hi, core).
Axes of the slice: x: 4, y: 8 (y_hi: 4, y_lo: 2; y = y_hi * 2 + y_lo), z: 16, core: 2. Of those that a mesh axis runs over, the one named last changes fastest.
Arguments:
- routes: int32 [4, 4096, 8], P('section', 'expert'), may hold values from 0 to 63, all different within a row; in each aligned block of 128 rows (0 to 127, 128 to 255, ..., all dimensions but the last counted through in order) at most 24 rows name the same one
- weights: float32 [4, 4096, 8], P('section', 'expert'), may hold values from 0.02 to 0.25
- cotangent: bfloat16 [4, 4096, 7168], P('section', 'expert', 'dp'), may hold values from -6 to 6
- hidden: bfloat16 [4, 64, 768, 1024], P('section', 'expert'), may hold values from -6 to 6
Outputs:
- grad: bfloat16 [2, 64, 1024, 7168], P(None, 'expert', None, ('dp', 'section'))
The draws below stay inside these ranges and needn't reach their ends.
Inputs may be any that keep to these rules, and one draw needn't show every extreme that they name: `routes`: in each aligned block of 128 token rows of a section, no expert is named more than 24 times, a bound that some block reaches.
All inputs are finite; a program needn't handle non-finite values.
Results may differ from the reference program's by a relative error of at most 0.0058.
Values may be sent and summed in bfloat16 or wider, within the bound.
A program may use at most 32 MiB of HBM per device.

```python
import math
import jax
import jax.numpy as jnp
import numpy as np
from jax import lax

D = 7168
TOP = 8
FFW = 1024
TOK_DEV = 128
EXPERTS = 64
TOKENS = 4096
C = 24
SLOTS = 768
N_SECTION = 4
N_EXPERT = 32


def levels(own_key, dims, cuts, least, high):
    loudness = 1.0
    for position, parts in cuts:
        steps = jax.random.uniform(jax.random.fold_in(jax.random.fold_in(own_key, 6), position), (parts,), jnp.float32, least / len(cuts), high / len(cuts))
        loudness = loudness * jnp.repeat(jnp.exp(steps), dims[position] // parts).reshape((-1,) + (1,) * (len(dims) - 1 - position))
    return loudness


def shared_out(rng, own, number, rows, amount, top, most, slope):
    sequence = jax.random.permutation(rng, amount)
    crowded, common = portions_of(amount, rows * top, most, slope, True), portions_of(amount, rows * top, most, slope, False)
    places = jnp.arange(amount)

    def named(tallies, turn):
        used = int((tallies > 0).sum())
        fixed = max(1, used // 4)
        passed = fixed + (places - fixed + turn * (used - fixed)) % max(1, amount - fixed)
        return jnp.zeros((amount,), jnp.int32).at[sequence[jnp.where(places < fixed, places, passed)]].set(jnp.asarray(tallies, jnp.int32))

    tallies = jnp.where(number % 4 == 0, named(crowded, number // 4), named(common, number - number // 4 - 1))
    mixed = jax.random.permutation(jax.random.fold_in(own, 3), amount)
    giver, taker = mixed[0:amount // 2 * 2:2], mixed[1:amount // 2 * 2:2]
    room = jnp.minimum(tallies[giver] - 1, most - tallies[taker]) // 2
    room = jnp.where((giver == sequence[0]) | (taker == sequence[0]) | (tallies[taker] == 0), 0, jnp.maximum(room, 0))
    passed = jax.random.randint(jax.random.fold_in(own, 4), (amount // 2,), 0, 1 << 20) % (room + 1)
    tallies = tallies.at[giver].add(-passed).at[taker].add(passed)
    items = jnp.searchsorted(jnp.cumsum(tallies), jnp.arange(rows * top), side="right").astype(jnp.int32)
    table = items.reshape(top, rows).T
    table = table[jax.random.permutation(jax.random.fold_in(own, 1), rows)]
    turn = jax.random.randint(jax.random.fold_in(own, 2), (rows, 1), 0, top)
    return jnp.take_along_axis(table, (jnp.arange(top)[None, :] + turn) % top, axis=1)


def portions_of(count, total, reach, lean, full):
    loads = [(1 << 20) // math.isqrt(standing ** lean) + 1 for standing in range(1, count + 1)]
    largest = reach if full else min(reach, max(-(-total // count), total * loads[0] // sum(loads)))
    least = 1 if total - largest >= count - 1 else 0
    given, spare = [largest] + [least] * (count - 1), total - largest - least * (count - 1)
    while spare > 0:
        free = [i for i in range(1, count) if given[i] < largest] or [i for i in range(1, count) if given[i] < reach]
        whole, remaining = sum([loads[i] for i in free]), spare
        for i in free:
            addition = min(reach - given[i], max(1, remaining * loads[i] // whole), spare)
            given[i] = given[i] + addition
            spare = spare - addition
    return np.array(given)


def noise(rng, shape, scale, most, split=(), held_as=jnp.bfloat16):
    array = jax.random.normal(rng, shape, jnp.float32) * scale
    if len(split) > 0:
        array = levels(rng, shape, split, -0.22, 0.18) * array
    return jnp.clip(array, min=-most, max=most).astype(held_as)


def setup_inputs(seed: int = 0) -> dict:
    arg_keys = jax.random.split(jax.random.key(seed), 5)
    routes_keys = jax.random.split(jax.random.fold_in(arg_keys[0], 1), N_SECTION * TOKENS // TOK_DEV)
    routes_turns = jax.random.permutation(jax.random.fold_in(arg_keys[0], 3), N_SECTION * TOKENS // TOK_DEV)
    routes = jax.vmap(lambda own, number: shared_out(jax.random.fold_in(arg_keys[0], 2), own, number, TOK_DEV, EXPERTS, TOP, C, 2))(routes_keys, routes_turns).reshape((N_SECTION, TOKENS, TOP))
    weights = jnp.clip(0.02 + 0.23 * jax.random.uniform(arg_keys[1], (N_SECTION, TOKENS, TOP), jnp.float32) ** levels(arg_keys[1], (N_SECTION, TOKENS, TOP), ((0, 4), (1, 32)), -0.2, 0.2), 0.02, 0.25)
    cotangent = noise(arg_keys[2], (N_SECTION, TOKENS, D), 1.0, 6.0, ((0, 4), (1, 32), (2, 8)))
    hidden = noise(arg_keys[3], (N_SECTION, EXPERTS, SLOTS, FFW), 1.0, 6.0, ((0, 4), (1, 32)))
    return dict(routes=routes, weights=weights, cotangent=cotangent, hidden=hidden)


def section_tables(routes):
    rows_block = TOK_DEV * TOP
    all_rows = TOKENS * TOP
    tables = []
    for section_num in range(N_SECTION):
        blocks = routes[section_num].reshape(N_EXPERT, rows_block)
        onehot = (blocks[:, :, None] == jnp.arange(EXPERTS, dtype=jnp.int32)[None, None, :]).astype(jnp.int32)
        earlier = jnp.cumsum(onehot, axis=1) - onehot
        ranks = lax.optimization_barrier(jnp.sum(earlier * onehot, axis=2)).astype(jnp.int32)
        slots = jnp.arange(N_EXPERT, dtype=jnp.int32)[:, None] * C + ranks
        table = jnp.full((EXPERTS, SLOTS), all_rows, jnp.int32)
        table = table.at[blocks.reshape(-1), slots.reshape(-1)].set(jnp.arange(all_rows, dtype=jnp.int32))
        tables.append(table)
    return tables

def reference(routes, weights, cotangent, hidden):
    tables = section_tables(routes)
    flat_weights = [jnp.concatenate([weights[s].reshape(-1), jnp.zeros((1,), jnp.float32)]) for s in range(N_SECTION)]
    padded = [jnp.concatenate([cotangent[s], jnp.zeros((1, D), cotangent.dtype)], axis=0) for s in range(N_SECTION)]

    def one_partial(entries, saved, section_num):
        token_idx = entries // TOP
        rows = (flat_weights[section_num][entries][:, None] * padded[section_num][token_idx].astype(jnp.float32)).astype(jnp.bfloat16)
        return jnp.dot(saved.T, rows, preferred_element_type=jnp.float32).astype(jnp.bfloat16)
    factor = 2.0 / math.sqrt(SLOTS)
    pairs = []
    for pair_num in range(N_SECTION // 2):
        mirror = N_SECTION - 1 - pair_num

        def per_expert(items):
            first = one_partial(items[0], items[2], pair_num).astype(jnp.float32)
            second = one_partial(items[1], items[3], mirror).astype(jnp.float32)
            return ((first + second) * factor).astype(jnp.bfloat16)
        pairs.append(lax.map(per_expert, (tables[pair_num], tables[mirror], hidden[pair_num], hidden[mirror])))
    return jnp.stack(pairs, axis=0)
```

```python
import functools
import math

import jax
import jax.numpy as jnp
from jax import lax
from jax.experimental import pallas as pl
from jax.experimental.pallas import tpu as pltpu
from jax.sharding import PartitionSpec as P

MESH = pl.DeviceIdType.MESH
BF = jnp.bfloat16
F32 = jnp.float32
LANE = 128
DEPTH = 3


def kernel(
    cfg,
    routes_ref,
    weights_ref,
    cot_ref,
    hid_ref,
    out_ref,
    cot_t,
    buf_a,
    buf_b,
    mir_a,
    hid_own,
    hid_mir,
    hid_t,
    upper,
    sel,
    scale,
    mine,
    other,
    routed,
    out_a,
    out_b,
    ring_s,
    ring_r,
    mir_s,
    mir_r,
    hid_l,
    hid_s,
    hid_r,
    sib_s,
    sib_r,
    pair_s,
    pair_r,
    lat_s,
    lat_r,
    out_l,
):
    half, cap, width, pieces, tops = cfg
    blocks = 2 * half
    rows = 2 * cap
    s = lax.axis_index("section")
    e = lax.axis_index("expert")
    d = lax.axis_index("dp")
    z = e // 2
    yl = lax.rem(e, 2)
    core = lax.rem(d, 2)
    n_exp = 2 * blocks
    up = {"expert": lax.rem(e + 2, n_exp)}
    down = {"expert": lax.rem(e + n_exp - 2, n_exp)}
    partner = {"expert": e + 1 - 2 * yl}
    sibling = {"dp": d + 1 - 2 * core}
    mirror_s = 3 - s
    mirror = {"section": mirror_s}
    lat_sec = s + 1 - 2 * lax.rem(s, 2)
    lateral = {"section": lat_sec}
    pair_index = jnp.where(s < 2, s, 3 - s)
    factor = 2.0 / math.sqrt(rows * blocks)
    bufs = (buf_a, buf_b)

    def remote(src, dst, ss, rs, where):
        return pltpu.make_async_remote_copy(
            src_ref=src, dst_ref=dst, send_sem=ss, recv_sem=rs, device_id=where, device_id_type=MESH
        )

    def ring(ch, way, sec, k):
        if way == 0:
            dst, src = 2 * k - 1, jnp.maximum(2 * k - 3, 0)
        else:
            dst, src = jnp.minimum(2 * k, blocks - 1), 2 * k - 2
        buf = bufs[ch]
        return remote(
            buf.at[sec, src],
            buf.at[sec, dst],
            ring_s.at[ch, way, sec, k],
            ring_r.at[ch, way, sec, k],
            up if way == 0 else down,
        )

    def hid_local(ex, f):
        return pltpu.make_async_copy(
            hid_ref.at[ex, :, pl.ds(pl.multiple_of(f * LANE, LANE), LANE)],
            hid_own.at[ex, f],
            hid_l.at[ex, f],
        )

    def hid_send(f):
        return remote(
            hid_ref.at[core, :, pl.ds(pl.multiple_of(f * LANE, LANE), LANE)],
            hid_mir.at[core, f],
            hid_s.at[f],
            hid_r.at[f],
            mirror,
        )

    def sib_send(f):
        return remote(hid_mir.at[core, f], hid_mir.at[core, f], sib_s.at[f], sib_r.at[f], sibling)

    def pair_copy(ch, k, first, count):
        return remote(
            other.at[ch, pl.ds(first, count)],
            mine.at[ch, yl, pl.ds(first, count)],
            pair_s.at[ch, k],
            pair_r.at[ch, k],
            partner,
        )

    def lat_send(f):
        return remote(
            out_a.at[f],
            out_ref.at[pair_index, :, pl.ds(pl.multiple_of(f * LANE, LANE), LANE), :],
            lat_s.at[f],
            lat_r.at[f],
            lateral,
        )

    barrier = pltpu.get_barrier_semaphore()
    for where in (up, down, partner, sibling, mirror, lateral):
        pl.semaphore_signal(barrier, inc=1, device_id=where, device_id_type=MESH)
    for ex in range(2):
        for f in range(pieces):
            hid_local(ex, f).start()
    cot_t[...] = cot_ref[...].T
    routes = routes_ref[...].astype(F32)
    w0 = weights_ref[...]
    w1 = w0.astype(BF)
    rest = w0 - w1.astype(F32)
    w2 = rest.astype(BF)
    w3 = (rest - w2.astype(F32)).astype(BF)
    info = jnp.concatenate(
        [routes, w1.astype(F32), w2.astype(F32), w3.astype(F32)], axis=0
    ).astype(BF)

    def columns(section):
        return cot_t[pl.ds(pl.multiple_of(section * width, 16), width), :]

    buf_a[0, 0, 0:width, :] = columns(lat_sec)
    buf_a[0, 0, width : width + 4 * tops, :] = info
    buf_b[0, 0] = columns(s)
    mir_a[0, 0:width, :] = columns(mirror_s + 1 - 2 * lax.rem(mirror_s, 2))
    mir_a[0, width : width + 4 * tops, :] = info
    mir_a[1, 0:width, :] = columns(mirror_s)
    row = lax.broadcasted_iota(jnp.int32, (LANE, LANE), 0)
    col = lax.broadcasted_iota(jnp.int32, (LANE, LANE), 1)
    upper[...] = jnp.where(row < col, 1.0, 0.0).astype(BF)
    pl.semaphore_wait(barrier, 6)

    mir_copies = (
        remote(mir_a.at[0], buf_a.at[1, 0], mir_s.at[0], mir_r.at[0], mirror),
        remote(mir_a.at[1, pl.ds(0, width)], buf_b.at[1, 0], mir_s.at[1], mir_r.at[1], mirror),
    )
    for copy in mir_copies:
        copy.start()
    for way in range(2):
        ring(0, way, 0, 1).start()
    for f in range(min(DEPTH, pieces)):
        hid_send(f).start()

    experts = [4 * z + 2 * yl, 4 * z + 2 * yl + 1, 4 * z + 2 - 2 * yl, 4 * z + 3 - 2 * yl]

    def build(slots):
        masks, gains, combos = [], [], [(sec, slot) for slot in slots for sec in range(2)]
        for sec, slot in combos:
            data = buf_a[sec, slot, width : width + 4 * tops, :].astype(F32)
            named = data[0:tops]
            gain = data[tops : 2 * tops] + data[2 * tops : 3 * tops] + data[3 * tops : 4 * tops]
            for ex in experts:
                hit = jnp.where(named == ex.astype(F32), 1.0, 0.0)
                masks.append(jnp.sum(hit, axis=0, keepdims=True))
                gains.append(jnp.sum(hit * gain, axis=0, keepdims=True))
        mask = jnp.concatenate(masks, axis=0)
        rank = jnp.dot(mask.astype(BF), upper[...], preferred_element_type=F32)
        rank = jnp.where(mask > 0.5, rank, -1.0)
        place = lax.broadcasted_iota(jnp.int32, (cap, LANE), 0).astype(F32)
        for i, (sec, slot) in enumerate(combos):
            hots, weights = [], []
            for j in range(4):
                n = 4 * i + j
                hot = place == rank[n : n + 1]
                hots.append(jnp.where(hot, 1.0, 0.0))
                one = jnp.sum(jnp.where(hot, gains[n], 0.0), axis=1, keepdims=True)
                weights.append(jnp.broadcast_to(one, (cap, LANE)))
            sel[sec, slot] = jnp.concatenate(hots, axis=0).astype(BF)
            scale[sec, slot] = jnp.concatenate(weights, axis=0)

    def pick(ch, slots):
        for slot in slots:
            for sec in range(2):
                hot = sel[sec, slot]
                data = bufs[ch][sec, slot, 0:width, :]
                got = lax.dot_general(
                    hot, data, (((1,), (1,)), ((), ())), preferred_element_type=F32
                )
                gain = scale[sec, slot]
                parts = -(-width // LANE)
                gain = jnp.concatenate([gain] * parts, axis=1)[:, :width]
                got = (got * gain).astype(BF)
                mine[ch, yl, slot, sec] = got[0:rows]
                other[ch, slot, sec] = got[rows : 2 * rows]

    def merge(ch, k, slots):
        pair_copy(ch, k, slots[0], len(slots)).wait()
        for slot in slots:
            for sec in range(2):
                first = mine[ch, 0, slot, sec].astype(F32)
                second = mine[ch, 1, slot, sec].astype(F32)
                at = pl.ds(pl.multiple_of(slot * rows, 16), rows)
                for ex in range(2):
                    part = slice(ex * cap, (ex + 1) * cap)
                    routed[ch, sec, ex, at, :] = jnp.concatenate(
                        [first[part], second[part]], axis=0
                    ).astype(BF)

    def turn(sec, ex, f, source):
        got = []
        for n in range(blocks):
            step = (n + 1) // 2
            sign = -1 if n % 2 == 1 else 1
            zz = lax.rem(z + sign * step + blocks, blocks)
            got.append(source[ex, f, pl.ds(pl.multiple_of(zz * rows, 16), rows), :])
        at = pl.ds(pl.multiple_of(f * LANE, LANE), LANE)
        hid_t[sec, ex, at, :] = jnp.concatenate(got, axis=0).T

    def turn_own(f):
        for ex in range(2):
            hid_local(ex, f).wait()
            turn(0, ex, f, hid_own)

    def product(ch, ex, at):
        total = None
        for sec in range(2):
            term = jnp.dot(hid_t[sec, ex, at, :], routed[ch, sec, ex], preferred_element_type=F32)
            total = term if total is None else total + term
        return (total * factor).astype(BF)

    def send_first(f):
        at = pl.ds(pl.multiple_of(f * LANE, LANE), LANE)
        for ex in range(2):
            out_a[f, ex] = product(0, ex, at)
        lat_send(f).start()

    def slots_of(k):
        return (2 * k - 1, 2 * k)

    def receive(ch, k, sends):
        for sec in range(2):
            for way in range(2):
                ring(ch, way, sec, k).wait_recv()
                if sends == 2 or (sends == 1 and way == sec):
                    ring(ch, way, sec, k + 1).start()

    def sent(ch, k):
        for sec in range(2):
            for way in range(2):
                ring(ch, way, sec, k).wait_send()

    def mirror_piece(f):
        copy = hid_send(f)
        copy.wait()
        sib_send(f).start()

    mir_copies[0].wait()
    for way in range(2):
        ring(0, way, 1, 1).start()
    build((0,))
    pick(0, (0,))
    pair_copy(0, 0, 0, 1).start()
    mir_copies[1].wait()

    def steps(ch, j, last):
        k = 2 * j + 1
        receive(ch, k, 1 if last else 2)
        if ch == 0:
            build(slots_of(k))
        pick(ch, slots_of(k))
        pair_copy(ch, k, slots_of(k)[0], 2).start()
        sent(ch, k)
        if last is True and half == 2:
            merge(ch, 0, (0,))
        elif last:
            merge(ch, k - 1, slots_of(k - 1))
        else:

            @pl.when(j == 0)
            def _():
                merge(ch, 0, (0,))

            @pl.when(j > 0)
            def _():
                merge(ch, k - 1, slots_of(k - 1))

        if ch == 0:
            turn_own(2 * j)
        else:
            send_first(2 * j)

        k = k + 1
        if last:
            for way in range(2):
                ring(ch, way, way, k).wait_recv()
            if ch == 0:
                for way in range(2):
                    for sec in range(2):
                        ring(1, way, sec, 1).start()
        else:
            receive(ch, k, 2)
        f = j if ch == 0 else pieces // 2 + j
        mirror_piece(f)
        if isinstance(f, int):
            if f + DEPTH < pieces:
                hid_send(f + DEPTH).start()
        elif ch == 0:

            @pl.when(f + DEPTH < pieces)
            def _():
                hid_send(f + DEPTH).start()
        else:

            @pl.when(f + DEPTH < pieces)
            def _():
                hid_send(f + DEPTH).start()

        at = (2 * half - 1,) if last else slots_of(k)
        if ch == 0:
            build(at)
        pick(ch, at)
        pair_copy(ch, k, at[0], len(at)).start()
        if last:
            for way in range(2):
                ring(ch, way, way, k).wait_send()
        else:
            sent(ch, k)
        merge(ch, k - 1, slots_of(k - 1))
        if ch == 0:
            turn_own(2 * j + 1)
        sib_send(f).wait()
        for ex in range(2):
            turn(1, ex, f, hid_mir)
        if ch == 1:
            send_first(2 * j + 1)

    def whole(ch):
        pairs = half // 2
        if pairs > 1:

            def body(j, carry):
                steps(ch, j, False)
                return carry

            lax.fori_loop(0, pairs - 1, body, 0)
        steps(ch, pairs - 1, True)

    whole(0)
    pick(1, (0,))
    pair_copy(1, 0, 0, 1).start()
    merge(0, half, (2 * half - 1,))

    whole(1)
    merge(1, half, (2 * half - 1,))

    def out_copy(f):
        at = pl.ds(pl.multiple_of(f * LANE, LANE), LANE)
        return pltpu.make_async_copy(
            out_b.at[f], out_ref.at[pair_index, :, at, :], out_l.at[f]
        )

    def finish(f, carry):
        at = pl.ds(pl.multiple_of(f * LANE, LANE), LANE)
        for ex in range(2):
            out_b[f, ex] = product(1, ex, at)
        out_copy(f).start()
        return carry

    lax.fori_loop(0, pieces, finish, 0)

    def close(f, carry):
        lat_send(f).wait()
        out_copy(f).wait()
        return carry

    lax.fori_loop(0, pieces, close, 0)


def local(routes, weights, cotangent, hidden):
    tokens = routes.shape[1]
    tops = routes.shape[2]
    slot_count, units = hidden.shape[2], hidden.shape[3]
    n_exp = lax.axis_size("expert")
    sections = lax.axis_size("section")
    cap = slot_count // n_exp
    rows = 2 * cap
    half = n_exp // 4
    blocks = 2 * half
    width = cotangent.shape[2] // sections
    pieces = units // LANE
    cfg = (half, cap, width, pieces, tops)
    vmem = pl.BlockSpec(memory_space=pltpu.VMEM)
    hbm = pl.BlockSpec(memory_space=pl.ANY)
    dma = pltpu.SemaphoreType.DMA
    return pl.pallas_call(
        functools.partial(kernel, cfg),
        out_shape=jax.ShapeDtypeStruct((2, 2, units, width), BF),
        in_specs=[vmem, vmem, vmem, hbm],
        out_specs=hbm,
        scratch_shapes=[
            pltpu.VMEM((sections * width, tokens), BF),
            pltpu.VMEM((2, blocks, width + 4 * tops, tokens), BF),
            pltpu.VMEM((2, blocks, width, tokens), BF),
            pltpu.VMEM((2, width + 4 * tops, tokens), BF),
            pltpu.VMEM((2, pieces, slot_count, LANE), BF),
            pltpu.VMEM((2, pieces, slot_count, LANE), BF),
            pltpu.VMEM((2, 2, units, slot_count), BF),
            pltpu.VMEM((tokens, tokens), BF),
            pltpu.VMEM((2, blocks, 2 * rows, tokens), BF),
            pltpu.VMEM((2, blocks, 2 * rows, tokens), F32),
            pltpu.VMEM((2, 2, blocks, 2, rows, width), BF),
            pltpu.VMEM((2, blocks, 2, rows, width), BF),
            pltpu.VMEM((2, 2, 2, slot_count, width), BF),
            pltpu.VMEM((pieces, 2, LANE, width), BF),
            pltpu.VMEM((pieces, 2, LANE, width), BF),
            dma((2, 2, 2, half + 1)),
            dma((2, 2, 2, half + 1)),
            dma((2,)),
            dma((2,)),
            dma((2, pieces)),
            dma((pieces,)),
            dma((pieces,)),
            dma((pieces,)),
            dma((pieces,)),
            dma((2, half + 1)),
            dma((2, half + 1)),
            dma((pieces,)),
            dma((pieces,)),
            dma((pieces,)),
        ],
        compiler_params=pltpu.CompilerParams(
            collective_id=0, has_side_effects=True, vmem_limit_bytes=52 * 1024 * 1024
        ),
        cost_estimate=pl.CostEstimate(
            flops=8 * units * slot_count * width * 4, bytes_accessed=8 << 20, transcendentals=0
        ),
    )(
        jnp.swapaxes(routes, 1, 2)[0],
        jnp.swapaxes(weights, 1, 2)[0],
        cotangent[0],
        hidden[0],
    )


def solution(mesh):
    return jax.shard_map(
        local,
        mesh=mesh,
        in_specs=(
            P("section", "expert", None),
            P("section", "expert", None),
            P("section", "expert", "dp"),
            P("section", "expert", None, None),
        ),
        out_specs=P(None, "expert", None, ("dp", "section")),
        check_vma=False,
    )
```

```python
import functools
import math

import jax
import jax.numpy as jnp
from jax import lax
from jax.experimental import pallas as pl
from jax.experimental.pallas import tpu as pltpu
from jax.sharding import PartitionSpec as P

MESH = pl.DeviceIdType.MESH
BF = jnp.bfloat16
F32 = jnp.float32
LANE = 128
DEPTH = 3


def kernel(
    cfg,
    routes_hbm,
    weights_hbm,
    cot_hbm,
    hid_ref,
    out_ref,
    routes_ref,
    weights_ref,
    cot_ref,
    arg_sem,
    cot_t,
    buf_a,
    buf_b,
    mir_a,
    hid_own,
    hid_mir,
    hid_t,
    upper,
    sel,
    scale,
    mine,
    other,
    routed,
    out_a,
    out_b,
    total,
    ring_s,
    ring_r,
    mir_s,
    mir_r,
    hid_l,
    hid_s,
    hid_r,
    sib_s,
    sib_r,
    pair_s,
    pair_r,
    lat_s,
    lat_r,
    out_l,
):
    half, cap, width, pieces, tops = cfg
    blocks = 2 * half
    rows = 2 * cap
    s = lax.axis_index("section")
    e = lax.axis_index("expert")
    d = lax.axis_index("dp")
    z = e // 2
    yl = lax.rem(e, 2)
    core = lax.rem(d, 2)
    n_exp = 2 * blocks
    up = {"expert": lax.rem(e + 2, n_exp)}
    down = {"expert": lax.rem(e + n_exp - 2, n_exp)}
    partner = {"expert": e + 1 - 2 * yl}
    sibling = {"dp": d + 1 - 2 * core}
    mirror_s = 3 - s
    mirror = {"section": mirror_s}
    lat_sec = s + 1 - 2 * lax.rem(s, 2)
    lateral = {"section": lat_sec}
    pair_index = jnp.where(s < 2, s, 3 - s)
    factor = 2.0 / math.sqrt(rows * blocks)
    bufs = (buf_a, buf_b)

    def remote(src, dst, ss, rs, where):
        return pltpu.make_async_remote_copy(
            src_ref=src, dst_ref=dst, send_sem=ss, recv_sem=rs, device_id=where, device_id_type=MESH
        )

    def ring(ch, way, sec, k, h):
        if way == 0:
            dst, src = 2 * k - 1, jnp.maximum(2 * k - 3, 0)
        else:
            dst, src = jnp.minimum(2 * k, blocks - 1), 2 * k - 2
        buf = bufs[ch]
        count = (width + 4 * tops if ch == 0 else width) // 2
        part = pl.ds(h * count, count)
        return remote(
            buf.at[sec, src, part],
            buf.at[sec, dst, part],
            ring_s.at[ch, way, sec, k, h],
            ring_r.at[ch, way, sec, k, h],
            up if way == 0 else down,
        )

    def hid_local(ex, f):
        return pltpu.make_async_copy(
            hid_ref.at[ex, :, pl.ds(pl.multiple_of(f * LANE, LANE), LANE)],
            hid_own.at[ex, f],
            hid_l.at[ex, f],
        )

    def hid_send(f):
        return remote(
            hid_ref.at[core, :, pl.ds(pl.multiple_of(f * LANE, LANE), LANE)],
            hid_mir.at[core, f],
            hid_s.at[f],
            hid_r.at[f],
            mirror,
        )

    def sib_send(f):
        return remote(hid_mir.at[core, f], hid_mir.at[core, f], sib_s.at[f], sib_r.at[f], sibling)

    def pair_copy(ch, k, first, count):
        return remote(
            other.at[ch, pl.ds(first, count)],
            mine.at[ch, yl, pl.ds(first, count)],
            pair_s.at[ch, k],
            pair_r.at[ch, k],
            partner,
        )

    def lat_send(f):
        return remote(
            out_a.at[f],
            out_ref.at[pair_index, :, :, pl.ds(pl.multiple_of(f * LANE, LANE), LANE)],
            lat_s.at[f],
            lat_r.at[f],
            lateral,
        )

    barrier = pltpu.get_barrier_semaphore()
    for where in (up, down, partner, sibling, mirror, lateral):
        pl.semaphore_signal(barrier, inc=1, device_id=where, device_id_type=MESH)
    loads = [
        pltpu.make_async_copy(src, dst, arg_sem.at[i])
        for i, (src, dst) in enumerate(
            ((cot_hbm, cot_ref), (routes_hbm, routes_ref), (weights_hbm, weights_ref))
        )
    ]
    for load in loads:
        load.start()
    for load in loads:
        load.wait()
    for ex in range(2):
        for f in range(pieces):
            hid_local(ex, f).start()
    cot_t[...] = cot_ref[...].T
    routes = routes_ref[...].astype(F32)
    w0 = weights_ref[...]
    w1 = w0.astype(BF)
    rest = w0 - w1.astype(F32)
    w2 = rest.astype(BF)
    w3 = (rest - w2.astype(F32)).astype(BF)
    info = jnp.concatenate(
        [routes, w1.astype(F32), w2.astype(F32), w3.astype(F32)], axis=0
    ).astype(BF)

    def columns(section):
        return cot_t[pl.ds(pl.multiple_of(section * width, 16), width), :]

    buf_a[0, 0, 0:width, :] = columns(lat_sec)
    buf_a[0, 0, width : width + 4 * tops, :] = info
    buf_b[0, 0] = columns(s)
    mir_a[0, 0:width, :] = columns(mirror_s + 1 - 2 * lax.rem(mirror_s, 2))
    mir_a[0, width : width + 4 * tops, :] = info
    mir_a[1, 0:width, :] = columns(mirror_s)
    row = lax.broadcasted_iota(jnp.int32, (LANE, LANE), 0)
    col = lax.broadcasted_iota(jnp.int32, (LANE, LANE), 1)
    upper[...] = jnp.where(row < col, 1.0, 0.0).astype(BF)
    pl.semaphore_wait(barrier, 6)

    mir_copies = (
        remote(mir_a.at[0], buf_a.at[1, 0], mir_s.at[0], mir_r.at[0], mirror),
        remote(mir_a.at[1, pl.ds(0, width)], buf_b.at[1, 0], mir_s.at[1], mir_r.at[1], mirror),
    )
    mir_copies[0].start()
    for h in range(2):
        for way in range(2):
            ring(0, way, 0, 1, h).start()

    experts = [4 * z + 2 * yl, 4 * z + 2 * yl + 1, 4 * z + 2 - 2 * yl, 4 * z + 3 - 2 * yl]

    def build(slots):
        masks, gains, combos = [], [], [(sec, slot) for slot in slots for sec in range(2)]
        for sec, slot in combos:
            data = buf_a[sec, slot, width : width + 4 * tops, :].astype(F32)
            named = data[0:tops]
            gain = data[tops : 2 * tops] + data[2 * tops : 3 * tops] + data[3 * tops : 4 * tops]
            for ex in experts:
                hit = jnp.where(named == ex.astype(F32), 1.0, 0.0)
                masks.append(jnp.sum(hit, axis=0, keepdims=True))
                gains.append(jnp.sum(hit * gain, axis=0, keepdims=True))
        mask = jnp.concatenate(masks, axis=0)
        rank = jnp.dot(mask.astype(BF), upper[...], preferred_element_type=F32)
        rank = jnp.where(mask > 0.5, rank, -1.0)
        place = lax.broadcasted_iota(jnp.int32, (cap, LANE), 0).astype(F32)
        for i, (sec, slot) in enumerate(combos):
            hots, weights = [], []
            for j in range(4):
                n = 4 * i + j
                hot = place == rank[n : n + 1]
                hots.append(jnp.where(hot, 1.0, 0.0))
                one = jnp.sum(jnp.where(hot, gains[n], 0.0), axis=1, keepdims=True)
                weights.append(jnp.broadcast_to(one, (cap, LANE)))
            sel[sec, slot] = jnp.concatenate(hots, axis=0).astype(BF)
            scale[sec, slot] = jnp.concatenate(weights, axis=0)

    def pick(ch, slots):
        for slot in slots:
            for sec in range(2):
                hot = sel[sec, slot]
                data = bufs[ch][sec, slot, 0:width, :]
                got = lax.dot_general(
                    hot, data, (((1,), (1,)), ((), ())), preferred_element_type=F32
                )
                gain = scale[sec, slot]
                parts = -(-width // LANE)
                gain = jnp.concatenate([gain] * parts, axis=1)[:, :width]
                got = (got * gain).astype(BF)
                mine[ch, yl, slot, sec] = got[0:rows]
                other[ch, slot, sec] = got[rows : 2 * rows]

    def merge(ch, k, slots):
        pair_copy(ch, k, slots[0], len(slots)).wait()
        for slot in slots:
            for sec in range(2):
                first = mine[ch, 0, slot, sec].astype(F32)
                second = mine[ch, 1, slot, sec].astype(F32)
                at = pl.ds(pl.multiple_of(slot * rows, 16), rows)
                for ex in range(2):
                    part = slice(ex * cap, (ex + 1) * cap)
                    routed[ch, sec, ex, at, :] = jnp.concatenate(
                        [first[part], second[part]], axis=0
                    ).astype(BF)

    def turn(sec, ex, f, source):
        got = []
        for n in range(blocks):
            step = (n + 1) // 2
            sign = -1 if n % 2 == 1 else 1
            zz = lax.rem(z + sign * step + blocks, blocks)
            got.append(source[ex, f, pl.ds(pl.multiple_of(zz * rows, 16), rows), :])
        at = pl.ds(pl.multiple_of(f * LANE, LANE), LANE)
        hid_t[sec, ex, at, :] = jnp.concatenate(got, axis=0).T

    def turn_own(f):
        for ex in range(2):
            hid_local(ex, f).wait()
            turn(0, ex, f, hid_own)

    def product(ch, ex, at, depth):
        amount = None
        for sec in range(2):
            term = jnp.dot(
                hid_t[sec, ex, at, depth], routed[ch, sec, ex, depth, :], preferred_element_type=F32
            )
            amount = term if amount is None else amount + term
        return amount

    early_rows = (2 * half - 5) * rows // LANE * LANE
    wide = 2 * LANE

    def begin(f, carry):
        at = pl.ds(pl.multiple_of(f * wide, wide), wide)
        for ex in range(2):
            total[ex, at, :] = product(1, ex, at, slice(0, early_rows))
        return carry

    def send_first(f):
        at = pl.ds(pl.multiple_of(f * LANE, LANE), LANE)
        for ex in range(2):
            out_a[f, ex] = (product(0, ex, at, slice(None)) * factor).astype(BF).T
        lat_send(f).start()

    def slots_of(k):
        return (2 * k - 1, 2 * k)

    def receive(ch, k, sends):
        for sec in range(2):
            for h in range(2):
                for way in range(2):
                    if sends == 0 and way != sec:
                        continue
                    ring(ch, way, sec, k, h).wait_recv()
                    if sends == 2 or (sends == 1 and way == sec):
                        ring(ch, way, sec, k + 1, h).start()

    def sent(ch, k, far=False):
        for sec in range(2):
            for h in range(2):
                for way in range(2):
                    if not far or way == sec:
                        ring(ch, way, sec, k, h).wait_send()

    def when(condition, action):
        if isinstance(condition, bool):
            if condition:
                action()
        else:
            pl.when(condition)(action)

    def mirror_piece(f):
        hid_send(f).wait()
        sib_send(f).start()
        when(f + DEPTH < pieces, lambda: hid_send(f + DEPTH).start())

    def turn_piece(f):
        sib_send(f).wait()
        for ex in range(2):
            turn(1, ex, f, hid_mir)

    mir_copies[0].wait()
    for h in range(2):
        for way in range(2):
            ring(0, way, 1, 1, h).start()
    mir_copies[1].start()
    for f in range(min(DEPTH, pieces)):
        hid_send(f).start()
    build((0,))
    pick(0, (0,))
    pair_copy(0, 0, 0, 1).start()

    pairs = half // 2
    lead = pairs // 2

    def early(j, h):
        sec, k = j % 2 if isinstance(j, int) else lax.rem(j, 2), j // 2 + 1
        if isinstance(j, int):
            if k >= 2:
                for way in range(2):
                    ring(1, way, sec, k - 1, h).wait_recv()
        else:

            @pl.when(k >= 2)
            def _():
                for way in range(2):
                    ring(1, way, sec, k - 1, h).wait_recv()

        for way in range(2):
            ring(1, way, sec, k, h).start()

    def steps(ch, j, last):
        k = 2 * j + 1
        if ch == 0:
            receive(ch, k, 1 if last else 2)
            when(j == 1, lambda: mir_copies[1].wait())
            early(j, 0)
        elif isinstance(j, int):
            if k >= lead:
                receive(ch, k, 1 if last else 2)
        else:
            when(k >= lead, lambda: receive(ch, k, 1 if last else 2))
        if ch == 0:
            build(slots_of(k))
        pick(ch, slots_of(k))
        pair_copy(ch, k, slots_of(k)[0], 2).start()
        when(k >= 3, lambda: merge(ch, k - 2, slots_of(k - 2)))
        if ch == 0:
            when(j >= 2, lambda: turn_piece(j - 2))
            turn_own(2 * j)
        else:
            piece = pairs - 1 + 2 * j
            when(piece - 1 < pieces, lambda: turn_piece(piece - 1))
            when(piece < pieces, lambda: mirror_piece(piece))

            def rest_of_first():
                merge(0, half - 1, slots_of(half - 1))
                merge(0, half, (2 * half - 1,))

            when(j == 0, rest_of_first)
            more = (3 * j - 1 < pieces) if isinstance(j, int) else (j >= 1) & (3 * j - 1 < pieces)
            if not isinstance(j, int) or j >= 1:
                when(more, lambda: send_first(3 * j - 1))
            if last:
                lax.fori_loop(0, pieces // 2, begin, 0)
        sent(ch, k)

        k = k + 1
        receive(ch, k, 0 if last else 2)
        if ch == 0:
            early(j, 1)
        at = (2 * half - 1,) if last else slots_of(k)
        if ch == 0:
            build(at)
        pick(ch, at)
        pair_copy(ch, k, at[0], len(at)).start()
        when(j == 0, lambda: merge(ch, 0, (0,)))
        when(j >= 1, lambda: merge(ch, k - 2, slots_of(k - 2)))
        if ch == 0:
            when(j >= 1, lambda: mirror_piece(j - 1))
            turn_own(2 * j + 1)
        else:
            when(piece < pieces, lambda: turn_piece(piece))
            when(piece + 1 < pieces, lambda: mirror_piece(piece + 1))
            when(3 * j < pieces, lambda: send_first(3 * j))
            when(3 * j + 1 < pieces, lambda: send_first(3 * j + 1))
        sent(ch, k, far=last)

    def whole(ch):
        if pairs > 1:

            def body(j, carry):
                steps(ch, j, False)
                return carry

            lax.fori_loop(0, pairs - 1, body, 0)
        steps(ch, pairs - 1, True)

    whole(0)
    pick(1, (0,))
    pair_copy(1, 0, 0, 1).start()

    whole(1)
    merge(1, half - 1, slots_of(half - 1))
    merge(1, half, (2 * half - 1,))

    def out_copy(f):
        at = pl.ds(pl.multiple_of(f * wide, wide), wide)
        return pltpu.make_async_copy(
            out_b.at[f], out_ref.at[pair_index, :, :, at], out_l.at[f]
        )

    def finish(f, carry):
        at = pl.ds(pl.multiple_of(f * wide, wide), wide)
        for ex in range(2):
            late = total[ex, at, :] + product(1, ex, at, slice(early_rows, blocks * rows))
            out_b[f, ex] = (late * factor).astype(BF).T
        out_copy(f).start()
        return carry

    lax.fori_loop(0, pieces // 2, finish, 0)

    def close(f, carry):
        lat_send(f).wait()
        return carry

    lax.fori_loop(0, pieces, close, 0)

    def close_own(f, carry):
        out_copy(f).wait()
        return carry

    lax.fori_loop(0, pieces // 2, close_own, 0)


def local(routes, weights, cotangent, hidden):
    tokens = routes.shape[1]
    tops = routes.shape[2]
    slot_count, units = hidden.shape[2], hidden.shape[3]
    n_exp = lax.axis_size("expert")
    sections = lax.axis_size("section")
    cap = slot_count // n_exp
    rows = 2 * cap
    half = n_exp // 4
    blocks = 2 * half
    width = cotangent.shape[2] // sections
    pieces = units // LANE
    cfg = (half, cap, width, pieces, tops)
    hbm = pl.BlockSpec(memory_space=pl.ANY)
    dma = pltpu.SemaphoreType.DMA
    grad = pl.pallas_call(
        functools.partial(kernel, cfg),
        out_shape=jax.ShapeDtypeStruct((2, 2, width, units), BF),
        in_specs=[hbm, hbm, hbm, hbm],
        out_specs=hbm,
        scratch_shapes=[
            pltpu.VMEM((tops, tokens), jnp.int32),
            pltpu.VMEM((tops, tokens), F32),
            pltpu.VMEM((tokens, sections * width), BF),
            dma((3,)),
            pltpu.VMEM((sections * width, tokens), BF),
            pltpu.VMEM((2, blocks, width + 4 * tops, tokens), BF),
            pltpu.VMEM((2, blocks, width, tokens), BF),
            pltpu.VMEM((2, width + 4 * tops, tokens), BF),
            pltpu.VMEM((2, pieces, slot_count, LANE), BF),
            pltpu.VMEM((2, pieces, slot_count, LANE), BF),
            pltpu.VMEM((2, 2, units, slot_count), BF),
            pltpu.VMEM((tokens, tokens), BF),
            pltpu.VMEM((2, blocks, 2 * rows, tokens), BF),
            pltpu.VMEM((2, blocks, 2 * rows, tokens), F32),
            pltpu.VMEM((2, 2, blocks, 2, rows, width), BF),
            pltpu.VMEM((2, blocks, 2, rows, width), BF),
            pltpu.VMEM((2, 2, 2, slot_count, width), BF),
            pltpu.VMEM((pieces, 2, width, LANE), BF),
            pltpu.VMEM((pieces // 2, 2, width, 2 * LANE), BF),
            pltpu.VMEM((2, units, width), F32),
            dma((2, 2, 2, half + 1, 2)),
            dma((2, 2, 2, half + 1, 2)),
            dma((2,)),
            dma((2,)),
            dma((2, pieces)),
            dma((pieces,)),
            dma((pieces,)),
            dma((pieces,)),
            dma((pieces,)),
            dma((2, half + 1)),
            dma((2, half + 1)),
            dma((pieces,)),
            dma((pieces,)),
            dma((pieces // 2,)),
        ],
        compiler_params=pltpu.CompilerParams(
            collective_id=0, has_side_effects=True, vmem_limit_bytes=63 * 1024 * 1024
        ),
        cost_estimate=pl.CostEstimate(
            flops=8 * units * slot_count * width * 4, bytes_accessed=8 << 20, transcendentals=0
        ),
    )(
        jnp.swapaxes(routes, 1, 2)[0],
        jnp.swapaxes(weights, 1, 2)[0],
        cotangent[0],
        hidden[0],
    )
    return jnp.swapaxes(grad, 2, 3)


def solution(mesh):
    return jax.shard_map(
        local,
        mesh=mesh,
        in_specs=(
            P("section", "expert", None),
            P("section", "expert", None),
            P("section", "expert", "dp"),
            P("section", "expert", None, None),
        ),
        out_specs=P(None, "expert", None, ("dp", "section")),
        check_vma=False,
    )
```

```python
import functools
import math

import jax
import jax.numpy as jnp
from jax import lax
from jax.experimental import pallas as pl
from jax.experimental.pallas import tpu as pltpu
from jax.sharding import PartitionSpec as P

MESH = pl.DeviceIdType.MESH
BF = jnp.bfloat16
F32 = jnp.float32
LANE = 128
DEPTH = 3


def kernel(
    cfg,
    routes_hbm,
    weights_hbm,
    cot_hbm,
    hid_ref,
    out_ref,
    routes_ref,
    weights_ref,
    cot_ref,
    arg_sem,
    cot_t,
    buf_a,
    buf_b,
    mir_a,
    hid_own,
    hid_mir,
    hid_t,
    upper,
    sel,
    scale,
    mine,
    other,
    routed,
    out_a,
    out_b,
    total,
    ring_s,
    ring_r,
    mir_s,
    mir_r,
    hid_l,
    hid_s,
    hid_r,
    sib_s,
    sib_r,
    pair_s,
    pair_r,
    lat_s,
    lat_r,
    out_l,
):
    half, cap, width, pieces, tops = cfg
    blocks = 2 * half
    rows = 2 * cap
    s = lax.axis_index("section")
    e = lax.axis_index("expert")
    d = lax.axis_index("dp")
    z = e // 2
    yl = lax.rem(e, 2)
    core = lax.rem(d, 2)
    n_exp = 2 * blocks
    up = {"expert": lax.rem(e + 2, n_exp)}
    down = {"expert": lax.rem(e + n_exp - 2, n_exp)}
    partner = {"expert": e + 1 - 2 * yl}
    sibling = {"dp": d + 1 - 2 * core}
    mirror_s = 3 - s
    mirror = {"section": mirror_s}
    lat_sec = s + 1 - 2 * lax.rem(s, 2)
    lateral = {"section": lat_sec}
    pair_index = jnp.where(s < 2, s, 3 - s)
    factor = 2.0 / math.sqrt(rows * blocks)
    bufs = (buf_a, buf_b)

    def remote(src, dst, ss, rs, where):
        return pltpu.make_async_remote_copy(
            src_ref=src, dst_ref=dst, send_sem=ss, recv_sem=rs, device_id=where, device_id_type=MESH
        )

    def half_of(ch, h):
        total_rows = width + 2 * tops if ch == 0 else width
        first = (total_rows // 2 + 15) // 16 * 16
        return pl.ds(0, first) if h == 0 else pl.ds(first, total_rows - first)

    def ring(ch, way, sec, k, h):
        if way == 0:
            dst, src = 2 * k - 1, jnp.maximum(2 * k - 3, 0)
        else:
            dst, src = jnp.minimum(2 * k, blocks - 1), 2 * k - 2
        buf = bufs[ch]
        part = half_of(ch, h)
        return remote(
            buf.at[sec, src, part],
            buf.at[sec, dst, part],
            ring_s.at[ch, way, sec, k, h],
            ring_r.at[ch, way, sec, k, h],
            up if way == 0 else down,
        )

    def hid_local(ex, f):
        return pltpu.make_async_copy(
            hid_ref.at[ex, :, pl.ds(pl.multiple_of(f * LANE, LANE), LANE)],
            hid_own.at[ex, f],
            hid_l.at[ex, f],
        )

    def hid_send(f):
        return remote(
            hid_ref.at[core, :, pl.ds(pl.multiple_of(f * LANE, LANE), LANE)],
            hid_mir.at[core, f],
            hid_s.at[f],
            hid_r.at[f],
            mirror,
        )

    def sib_send(f):
        return remote(hid_mir.at[core, f], hid_mir.at[core, f], sib_s.at[f], sib_r.at[f], sibling)

    def pair_copy(ch, k, first, count):
        return remote(
            other.at[ch, pl.ds(first, count)],
            mine.at[ch, yl, pl.ds(first, count)],
            pair_s.at[ch, k],
            pair_r.at[ch, k],
            partner,
        )

    def lat_send(f):
        return remote(
            out_a.at[f],
            out_ref.at[pair_index, :, :, pl.ds(pl.multiple_of(f * LANE, LANE), LANE)],
            lat_s.at[f],
            lat_r.at[f],
            lateral,
        )

    barrier = pltpu.get_barrier_semaphore()
    for where in (up, down, partner, sibling, mirror, lateral):
        pl.semaphore_signal(barrier, inc=1, device_id=where, device_id_type=MESH)
    loads = [
        pltpu.make_async_copy(src, dst, arg_sem.at[i])
        for i, (src, dst) in enumerate(
            ((cot_hbm, cot_ref), (routes_hbm, routes_ref), (weights_hbm, weights_ref))
        )
    ]
    for load in loads:
        load.start()
    for load in loads:
        load.wait()
    cot_t[...] = cot_ref[...].T
    routes = routes_ref[...].astype(F32)
    info = jnp.concatenate([routes, weights_ref[...]], axis=0).astype(BF)

    def columns(section):
        return cot_t[pl.ds(pl.multiple_of(section * width, 16), width), :]

    buf_a[0, 0, 0:width, :] = columns(lat_sec)
    buf_a[0, 0, width : width + 2 * tops, :] = info
    buf_b[0, 0] = columns(s)
    mir_a[0, 0:width, :] = columns(mirror_s + 1 - 2 * lax.rem(mirror_s, 2))
    mir_a[0, width : width + 2 * tops, :] = info
    mir_a[1, 0:width, :] = columns(mirror_s)
    row = lax.broadcasted_iota(jnp.int32, (LANE, LANE), 0)
    col = lax.broadcasted_iota(jnp.int32, (LANE, LANE), 1)
    upper[...] = jnp.where(row < col, 1.0, 0.0).astype(BF)
    pl.semaphore_wait(barrier, 6)

    mir_first = [
        remote(
            mir_a.at[0, half_of(0, h)],
            buf_a.at[1, 0, half_of(0, h)],
            mir_s.at[h],
            mir_r.at[h],
            mirror,
        )
        for h in range(2)
    ]
    mir_second = remote(
        mir_a.at[1, pl.ds(0, width)], buf_b.at[1, 0], mir_s.at[2], mir_r.at[2], mirror
    )
    for h in range(2):
        mir_first[h].start()
        for way in range(2):
            ring(0, way, 0, 1, h).start()
    for ex in range(2):
        for f in range(pieces):
            hid_local(ex, f).start()

    experts = [4 * z + 2 * yl, 4 * z + 2 * yl + 1, 4 * z + 2 - 2 * yl, 4 * z + 3 - 2 * yl]

    def build(slots):
        masks, gains, combos = [], [], [(sec, slot) for slot in slots for sec in range(2)]
        for sec, slot in combos:
            data = buf_a[sec, slot, width : width + 2 * tops, :].astype(F32)
            named = data[0:tops]
            gain = data[tops : 2 * tops]
            for ex in experts:
                hit = jnp.where(named == ex.astype(F32), 1.0, 0.0)
                masks.append(jnp.sum(hit, axis=0, keepdims=True))
                gains.append(jnp.sum(hit * gain, axis=0, keepdims=True))
        mask = jnp.concatenate(masks, axis=0)
        rank = jnp.dot(mask.astype(BF), upper[...], preferred_element_type=F32)
        rank = jnp.where(mask > 0.5, rank, -1.0)
        place = lax.broadcasted_iota(jnp.int32, (cap, LANE), 0).astype(F32)
        for i, (sec, slot) in enumerate(combos):
            hots, weights = [], []
            for j in range(4):
                n = 4 * i + j
                hot = place == rank[n : n + 1]
                hots.append(jnp.where(hot, 1.0, 0.0))
                one = jnp.sum(jnp.where(hot, gains[n], 0.0), axis=1, keepdims=True)
                weights.append(jnp.broadcast_to(one, (cap, LANE)))
            sel[sec, slot] = jnp.concatenate(hots, axis=0).astype(BF)
            scale[sec, slot] = jnp.concatenate(weights, axis=0)

    def pick(ch, slots):
        for slot in slots:
            for sec in range(2):
                hot = sel[sec, slot]
                data = bufs[ch][sec, slot, 0:width, :]
                got = lax.dot_general(
                    hot, data, (((1,), (1,)), ((), ())), preferred_element_type=F32
                )
                gain = scale[sec, slot]
                parts = -(-width // LANE)
                gain = jnp.concatenate([gain] * parts, axis=1)[:, :width]
                got = (got * gain).astype(BF)
                mine[ch, yl, slot, sec] = got[0:rows]
                other[ch, slot, sec] = got[rows : 2 * rows]

    def merge(ch, k, slots):
        pair_copy(ch, k, slots[0], len(slots)).wait()
        for slot in slots:
            for sec in range(2):
                first = mine[ch, 0, slot, sec].astype(F32)
                second = mine[ch, 1, slot, sec].astype(F32)
                at = pl.ds(pl.multiple_of(slot * rows, 16), rows)
                for ex in range(2):
                    part = slice(ex * cap, (ex + 1) * cap)
                    routed[ch, sec, ex, at, :] = jnp.concatenate(
                        [first[part], second[part]], axis=0
                    ).astype(BF)

    def turn(sec, ex, f, source):
        got = []
        for n in range(blocks):
            step = (n + 1) // 2
            sign = -1 if n % 2 == 1 else 1
            zz = lax.rem(z + sign * step + blocks, blocks)
            got.append(source[ex, f, pl.ds(pl.multiple_of(zz * rows, 16), rows), :])
        at = pl.ds(pl.multiple_of(f * LANE, LANE), LANE)
        hid_t[sec, ex, at, :] = jnp.concatenate(got, axis=0).T

    def turn_own(f):
        for ex in range(2):
            hid_local(ex, f).wait()
            turn(0, ex, f, hid_own)

    def product(ch, ex, at, depth):
        amount = None
        for sec in range(2):
            term = jnp.dot(
                hid_t[sec, ex, at, depth], routed[ch, sec, ex, depth, :], preferred_element_type=F32
            )
            amount = term if amount is None else amount + term
        return amount

    early_rows = (2 * half - 5) * rows // LANE * LANE
    wide = 2 * LANE

    def begin(f, carry):
        at = pl.ds(pl.multiple_of(f * wide, wide), wide)
        for ex in range(2):
            total[ex, at, :] = product(1, ex, at, slice(0, early_rows))
        return carry

    def send_first(f):
        at = pl.ds(pl.multiple_of(f * LANE, LANE), LANE)
        for ex in range(2):
            out_a[f, ex] = (product(0, ex, at, slice(None)) * factor).astype(BF).T
        lat_send(f).start()

    def slots_of(k):
        return (2 * k - 1, 2 * k)

    def receive(ch, k, sends):
        for sec in range(2):
            for h in range(2):
                for way in range(2):
                    if sends == 0 and way != sec:
                        continue
                    ring(ch, way, sec, k, h).wait_recv()
                    if sends == 2 or (sends == 1 and way == sec):
                        ring(ch, way, sec, k + 1, h).start()

    def sent(ch, k, far=False):
        for sec in range(2):
            for h in range(2):
                for way in range(2):
                    if not far or way == sec:
                        ring(ch, way, sec, k, h).wait_send()

    def when(condition, action):
        if isinstance(condition, bool):
            if condition:
                action()
        else:
            pl.when(condition)(action)

    def mirror_piece(f):
        hid_send(f).wait()
        sib_send(f).start()
        when(f + DEPTH < pieces, lambda: hid_send(f + DEPTH).start())

    def turn_piece(f):
        sib_send(f).wait()
        for ex in range(2):
            turn(1, ex, f, hid_mir)

    for h in range(2):
        mir_first[h].wait()
        for way in range(2):
            ring(0, way, 1, 1, h).start()
    mir_second.start()
    for f in range(min(DEPTH, pieces)):
        hid_send(f).start()
    build((0,))
    pick(0, (0,))
    pair_copy(0, 0, 0, 1).start()

    pairs = half // 2
    lead = pairs // 2

    def early(j, h):
        sec, k = j % 2 if isinstance(j, int) else lax.rem(j, 2), j // 2 + 1
        if isinstance(j, int):
            if k >= 2:
                for way in range(2):
                    ring(1, way, sec, k - 1, h).wait_recv()
        else:

            @pl.when(k >= 2)
            def _():
                for way in range(2):
                    ring(1, way, sec, k - 1, h).wait_recv()

        for way in range(2):
            ring(1, way, sec, k, h).start()

    def steps(ch, j, last):
        k = 2 * j + 1
        if ch == 0:
            receive(ch, k, 1 if last else 2)
            when(j == 1, lambda: mir_second.wait())
            early(j, 0)
        elif isinstance(j, int):
            if k >= lead:
                receive(ch, k, 1 if last else 2)
        else:
            when(k >= lead, lambda: receive(ch, k, 1 if last else 2))
        if ch == 0:
            build(slots_of(k))
        pick(ch, slots_of(k))
        pair_copy(ch, k, slots_of(k)[0], 2).start()
        when(k >= 3, lambda: merge(ch, k - 2, slots_of(k - 2)))
        if ch == 0:
            when(j >= 2, lambda: turn_piece(j - 2))
            turn_own(2 * j)
        else:
            piece = pairs - 1 + 2 * j
            when(piece - 1 < pieces, lambda: turn_piece(piece - 1))
            when(piece < pieces, lambda: mirror_piece(piece))

            def rest_of_first():
                merge(0, half - 1, slots_of(half - 1))
                merge(0, half, (2 * half - 1,))

            when(j == 0, rest_of_first)
            more = (3 * j - 1 < pieces) if isinstance(j, int) else (j >= 1) & (3 * j - 1 < pieces)
            if not isinstance(j, int) or j >= 1:
                when(more, lambda: send_first(3 * j - 1))
            if last:
                lax.fori_loop(0, pieces // 2, begin, 0)
        sent(ch, k)

        k = k + 1
        receive(ch, k, 0 if last else 2)
        if ch == 0:
            early(j, 1)
        at = (2 * half - 1,) if last else slots_of(k)
        if ch == 0:
            build(at)
        pick(ch, at)
        pair_copy(ch, k, at[0], len(at)).start()
        when(j == 0, lambda: merge(ch, 0, (0,)))
        when(j >= 1, lambda: merge(ch, k - 2, slots_of(k - 2)))
        if ch == 0:
            when(j >= 1, lambda: mirror_piece(j - 1))
            turn_own(2 * j + 1)
        else:
            when(piece < pieces, lambda: turn_piece(piece))
            when(piece + 1 < pieces, lambda: mirror_piece(piece + 1))
            when(3 * j < pieces, lambda: send_first(3 * j))
            when(3 * j + 1 < pieces, lambda: send_first(3 * j + 1))
        sent(ch, k, far=last)

    def whole(ch):
        if pairs > 1:

            def body(j, carry):
                steps(ch, j, False)
                return carry

            lax.fori_loop(0, pairs - 1, body, 0)
        steps(ch, pairs - 1, True)

    whole(0)
    pick(1, (0,))
    pair_copy(1, 0, 0, 1).start()

    whole(1)
    merge(1, half - 1, slots_of(half - 1))
    merge(1, half, (2 * half - 1,))

    def out_copy(f):
        at = pl.ds(pl.multiple_of(f * wide, wide), wide)
        return pltpu.make_async_copy(
            out_b.at[f], out_ref.at[pair_index, :, :, at], out_l.at[f]
        )

    def finish(f, carry):
        at = pl.ds(pl.multiple_of(f * wide, wide), wide)
        for ex in range(2):
            late = total[ex, at, :] + product(1, ex, at, slice(early_rows, blocks * rows))
            out_b[f, ex] = (late * factor).astype(BF).T
        out_copy(f).start()
        return carry

    lax.fori_loop(0, pieces // 2, finish, 0)

    def close(f, carry):
        lat_send(f).wait()
        return carry

    lax.fori_loop(0, pieces, close, 0)

    def close_own(f, carry):
        out_copy(f).wait()
        return carry

    lax.fori_loop(0, pieces // 2, close_own, 0)


def move(parts, src, dst, held, come, go):
    size = src.shape[2] // parts
    places = [
        (p, ex, pl.ds(i * size, size)) for p in range(2) for ex in range(2) for i in range(parts)
    ]
    reads = [
        pltpu.make_async_copy(src.at[at], held.at[at], come.at[i]) for i, at in enumerate(places)
    ]
    writes = [
        pltpu.make_async_copy(held.at[at], dst.at[at], go.at[i]) for i, at in enumerate(places)
    ]
    for read in reads:
        read.start()
    for read, write in zip(reads, writes):
        read.wait()
        write.start()
    for write in writes:
        write.wait()


def local(routes, weights, cotangent, hidden):
    tokens = routes.shape[1]
    tops = routes.shape[2]
    slot_count, units = hidden.shape[2], hidden.shape[3]
    n_exp = lax.axis_size("expert")
    sections = lax.axis_size("section")
    cap = slot_count // n_exp
    rows = 2 * cap
    half = n_exp // 4
    blocks = 2 * half
    width = cotangent.shape[2] // sections
    pieces = units // LANE
    cfg = (half, cap, width, pieces, tops)
    hbm = pl.BlockSpec(memory_space=pl.ANY)
    dma = pltpu.SemaphoreType.DMA
    grad = pl.pallas_call(
        functools.partial(kernel, cfg),
        out_shape=jax.ShapeDtypeStruct((2, 2, width, units), BF),
        in_specs=[hbm, hbm, hbm, hbm],
        out_specs=hbm,
        scratch_shapes=[
            pltpu.VMEM((tops, tokens), jnp.int32),
            pltpu.VMEM((tops, tokens), F32),
            pltpu.VMEM((tokens, sections * width), BF),
            dma((3,)),
            pltpu.VMEM((sections * width, tokens), BF),
            pltpu.VMEM((2, blocks, width + 2 * tops, tokens), BF),
            pltpu.VMEM((2, blocks, width, tokens), BF),
            pltpu.VMEM((2, width + 2 * tops, tokens), BF),
            pltpu.VMEM((2, pieces, slot_count, LANE), BF),
            pltpu.VMEM((2, pieces, slot_count, LANE), BF),
            pltpu.VMEM((2, 2, units, slot_count), BF),
            pltpu.VMEM((tokens, tokens), BF),
            pltpu.VMEM((2, blocks, 2 * rows, tokens), BF),
            pltpu.VMEM((2, blocks, 2 * rows, tokens), F32),
            pltpu.VMEM((2, 2, blocks, 2, rows, width), BF),
            pltpu.VMEM((2, blocks, 2, rows, width), BF),
            pltpu.VMEM((2, 2, 2, slot_count, width), BF),
            pltpu.VMEM((pieces, 2, width, LANE), BF),
            pltpu.VMEM((pieces // 2, 2, width, 2 * LANE), BF),
            pltpu.VMEM((2, units, width), F32),
            dma((2, 2, 2, half + 1, 2)),
            dma((2, 2, 2, half + 1, 2)),
            dma((3,)),
            dma((3,)),
            dma((2, pieces)),
            dma((pieces,)),
            dma((pieces,)),
            dma((pieces,)),
            dma((pieces,)),
            dma((2, half + 1)),
            dma((2, half + 1)),
            dma((pieces,)),
            dma((pieces,)),
            dma((pieces // 2,)),
        ],
        compiler_params=pltpu.CompilerParams(
            collective_id=0, has_side_effects=True, vmem_limit_bytes=63 * 1024 * 1024
        ),
        cost_estimate=pl.CostEstimate(
            flops=8 * units * slot_count * width * 4, bytes_accessed=8 << 20, transcendentals=0
        ),
    )(
        jnp.swapaxes(routes, 1, 2)[0],
        jnp.swapaxes(weights, 1, 2)[0],
        cotangent[0],
        hidden[0],
    )
    grad = pl.pallas_call(
        functools.partial(move, 2),
        out_shape=jax.ShapeDtypeStruct(grad.shape, grad.dtype),
        in_specs=[hbm],
        out_specs=hbm,
        scratch_shapes=[pltpu.VMEM(grad.shape, grad.dtype), dma((8,)), dma((8,))],
        compiler_params=pltpu.CompilerParams(vmem_limit_bytes=63 * 1024 * 1024),
    )(grad)
    return jnp.swapaxes(grad, 2, 3)


def solution(mesh):
    return jax.shard_map(
        local,
        mesh=mesh,
        in_specs=(
            P("section", "expert", None),
            P("section", "expert", None),
            P("section", "expert", "dp"),
            P("section", "expert", None, None),
        ),
        out_specs=P(None, "expert", None, ("dp", "section")),
        check_vma=False,
    )
```

```python
import functools
import math

import jax
import jax.numpy as jnp
from jax import lax
from jax.experimental import pallas as pl
from jax.experimental.pallas import tpu as pltpu
from jax.sharding import PartitionSpec as P

MESH = pl.DeviceIdType.MESH
BF = jnp.bfloat16
F32 = jnp.float32
LANE = 128
DEPTH = 3


def kernel(
    cfg,
    routes_hbm,
    weights_hbm,
    cot_hbm,
    hid_ref,
    out_ref,
    routes_ref,
    weights_ref,
    cot_ref,
    arg_sem,
    cot_t,
    buf_a,
    buf_b,
    mir_a,
    hid_own,
    hid_mir,
    hid_t,
    upper,
    sel,
    scale,
    mine,
    other,
    routed,
    out_a,
    out_b,
    total,
    ring_s,
    ring_r,
    mir_s,
    mir_r,
    hid_l,
    hid_s,
    hid_r,
    sib_s,
    sib_r,
    pair_s,
    pair_r,
    lat_s,
    lat_r,
    out_l,
):
    half, cap, width, pieces, tops = cfg
    blocks = 2 * half
    rows = 2 * cap
    s = lax.axis_index("section")
    e = lax.axis_index("expert")
    d = lax.axis_index("dp")
    z = e // 2
    yl = lax.rem(e, 2)
    core = lax.rem(d, 2)
    n_exp = 2 * blocks
    up = {"expert": lax.rem(e + 2, n_exp)}
    down = {"expert": lax.rem(e + n_exp - 2, n_exp)}
    partner = {"expert": e + 1 - 2 * yl}
    sibling = {"dp": d + 1 - 2 * core}
    mirror_s = 3 - s
    mirror = {"section": mirror_s}
    lat_sec = s + 1 - 2 * lax.rem(s, 2)
    lateral = {"section": lat_sec}
    pair_index = jnp.where(s < 2, s, 3 - s)
    factor = 2.0 / math.sqrt(rows * blocks)
    bufs = (buf_a, buf_b)

    def remote(src, dst, ss, rs, where):
        return pltpu.make_async_remote_copy(
            src_ref=src, dst_ref=dst, send_sem=ss, recv_sem=rs, device_id=where, device_id_type=MESH
        )

    def half_of(ch, h):
        total_rows = width + 4 * tops if ch == 0 else width
        first = (total_rows // 2 + 15) // 16 * 16
        return pl.ds(0, first) if h == 0 else pl.ds(first, total_rows - first)

    def ring(ch, way, sec, k, h):
        if way == 0:
            dst, src = 2 * k - 1, jnp.maximum(2 * k - 3, 0)
        else:
            dst, src = jnp.minimum(2 * k, blocks - 1), 2 * k - 2
        buf = bufs[ch]
        part = half_of(ch, h)
        return remote(
            buf.at[sec, src, part],
            buf.at[sec, dst, part],
            ring_s.at[ch, way, sec, k, h],
            ring_r.at[ch, way, sec, k, h],
            up if way == 0 else down,
        )

    def hid_local(ex, f):
        return pltpu.make_async_copy(
            hid_ref.at[ex, :, pl.ds(pl.multiple_of(f * LANE, LANE), LANE)],
            hid_own.at[ex, f],
            hid_l.at[ex, f],
        )

    def hid_send(f):
        return remote(
            hid_ref.at[core, :, pl.ds(pl.multiple_of(f * LANE, LANE), LANE)],
            hid_mir.at[core, f],
            hid_s.at[f],
            hid_r.at[f],
            mirror,
        )

    def sib_send(f):
        return remote(hid_mir.at[core, f], hid_mir.at[core, f], sib_s.at[f], sib_r.at[f], sibling)

    def pair_copy(ch, k, first, count):
        return remote(
            other.at[ch, pl.ds(first, count)],
            mine.at[ch, yl, pl.ds(first, count)],
            pair_s.at[ch, k],
            pair_r.at[ch, k],
            partner,
        )

    def lat_send(f):
        return remote(
            out_a.at[f],
            out_ref.at[pair_index, :, :, pl.ds(pl.multiple_of(f * LANE, LANE), LANE)],
            lat_s.at[f],
            lat_r.at[f],
            lateral,
        )

    barrier = pltpu.get_barrier_semaphore()
    for where in (up, down, partner, sibling, mirror, lateral):
        pl.semaphore_signal(barrier, inc=1, device_id=where, device_id_type=MESH)
    loads = [
        pltpu.make_async_copy(src, dst, arg_sem.at[i])
        for i, (src, dst) in enumerate(
            ((cot_hbm, cot_ref), (routes_hbm, routes_ref), (weights_hbm, weights_ref))
        )
    ]
    for load in loads:
        load.start()
    for load in loads:
        load.wait()
    cot_t[...] = cot_ref[...].T
    routes = routes_ref[...].astype(F32)
    w0 = weights_ref[...]
    w1 = w0.astype(BF)
    rest = w0 - w1.astype(F32)
    w2 = rest.astype(BF)
    w3 = (rest - w2.astype(F32)).astype(BF)
    info = jnp.concatenate(
        [routes, w1.astype(F32), w2.astype(F32), w3.astype(F32)], axis=0
    ).astype(BF)

    def columns(section):
        return cot_t[pl.ds(pl.multiple_of(section * width, 16), width), :]

    buf_a[0, 0, 0:width, :] = columns(lat_sec)
    buf_a[0, 0, width : width + 4 * tops, :] = info
    buf_b[0, 0] = columns(s)
    mir_a[0, 0:width, :] = columns(mirror_s + 1 - 2 * lax.rem(mirror_s, 2))
    mir_a[0, width : width + 4 * tops, :] = info
    mir_a[1, 0:width, :] = columns(mirror_s)
    row = lax.broadcasted_iota(jnp.int32, (LANE, LANE), 0)
    col = lax.broadcasted_iota(jnp.int32, (LANE, LANE), 1)
    upper[...] = jnp.where(row < col, 1.0, 0.0).astype(BF)
    pl.semaphore_wait(barrier, 6)

    mir_first = [
        remote(
            mir_a.at[0, half_of(0, h)],
            buf_a.at[1, 0, half_of(0, h)],
            mir_s.at[h],
            mir_r.at[h],
            mirror,
        )
        for h in range(2)
    ]
    mir_second = remote(
        mir_a.at[1, pl.ds(0, width)], buf_b.at[1, 0], mir_s.at[2], mir_r.at[2], mirror
    )
    for h in range(2):
        mir_first[h].start()
        for way in range(2):
            ring(0, way, 0, 1, h).start()
    for ex in range(2):
        for f in range(pieces):
            hid_local(ex, f).start()

    experts = [4 * z + 2 * yl, 4 * z + 2 * yl + 1, 4 * z + 2 - 2 * yl, 4 * z + 3 - 2 * yl]

    def build(slots):
        masks, gains, combos = [], [], [(sec, slot) for slot in slots for sec in range(2)]
        for sec, slot in combos:
            data = buf_a[sec, slot, width : width + 4 * tops, :].astype(F32)
            named = data[0:tops]
            gain = data[tops : 2*tops] + data[2*tops : 3*tops] + data[3*tops : 4*tops]
            for ex in experts:
                hit = jnp.where(named == ex.astype(F32), 1.0, 0.0)
                masks.append(jnp.sum(hit, axis=0, keepdims=True))
                gains.append(jnp.sum(hit * gain, axis=0, keepdims=True))
        mask = jnp.concatenate(masks, axis=0)
        rank = jnp.dot(mask.astype(BF), upper[...], preferred_element_type=F32)
        rank = jnp.where(mask > 0.5, rank, -1.0)
        place = lax.broadcasted_iota(jnp.int32, (cap, LANE), 0).astype(F32)
        for i, (sec, slot) in enumerate(combos):
            hots, weights = [], []
            for j in range(4):
                n = 4 * i + j
                hot = place == rank[n : n + 1]
                hots.append(jnp.where(hot, 1.0, 0.0))
                one = jnp.sum(jnp.where(hot, gains[n], 0.0), axis=1, keepdims=True)
                weights.append(jnp.broadcast_to(one, (cap, LANE)))
            sel[sec, slot] = jnp.concatenate(hots, axis=0).astype(BF)
            scale[sec, slot] = jnp.concatenate(weights, axis=0)

    def pick(ch, slots):
        for slot in slots:
            for sec in range(2):
                hot = sel[sec, slot]
                data = bufs[ch][sec, slot, 0:width, :]
                got = lax.dot_general(
                    hot, data, (((1,), (1,)), ((), ())), preferred_element_type=F32
                )
                gain = scale[sec, slot]
                parts = -(-width // LANE)
                gain = jnp.concatenate([gain] * parts, axis=1)[:, :width]
                got = (got * gain).astype(BF)
                mine[ch, yl, slot, sec] = got[0:rows]
                other[ch, slot, sec] = got[rows : 2 * rows]

    def merge(ch, k, slots):
        pair_copy(ch, k, slots[0], len(slots)).wait()
        for slot in slots:
            for sec in range(2):
                first = mine[ch, 0, slot, sec].astype(F32)
                second = mine[ch, 1, slot, sec].astype(F32)
                at = pl.ds(pl.multiple_of(slot * rows, 16), rows)
                for ex in range(2):
                    part = slice(ex * cap, (ex + 1) * cap)
                    routed[ch, sec, ex, at, :] = jnp.concatenate(
                        [first[part], second[part]], axis=0
                    ).astype(BF)

    def turn(sec, ex, f, source):
        got = []
        for n in range(blocks):
            step = (n + 1) // 2
            sign = -1 if n % 2 == 1 else 1
            zz = lax.rem(z + sign * step + blocks, blocks)
            got.append(source[ex, f, pl.ds(pl.multiple_of(zz * rows, 16), rows), :])
        at = pl.ds(pl.multiple_of(f * LANE, LANE), LANE)
        hid_t[sec, ex, at, :] = jnp.concatenate(got, axis=0).T

    def turn_own(f):
        for ex in range(2):
            hid_local(ex, f).wait()
            turn(0, ex, f, hid_own)

    def product(ch, ex, at, depth):
        amount = None
        for sec in range(2):
            term = jnp.dot(
                hid_t[sec, ex, at, depth], routed[ch, sec, ex, depth, :], preferred_element_type=F32
            )
            amount = term if amount is None else amount + term
        return amount

    early_rows = (2 * half - 5) * rows // LANE * LANE
    wide = 2 * LANE

    def begin(f, carry):
        at = pl.ds(pl.multiple_of(f * wide, wide), wide)
        for ex in range(2):
            total[ex, at, :] = product(1, ex, at, slice(0, early_rows))
        return carry

    def send_first(f):
        at = pl.ds(pl.multiple_of(f * LANE, LANE), LANE)
        for ex in range(2):
            out_a[f, ex] = (product(0, ex, at, slice(None)) * factor).astype(BF).T
        lat_send(f).start()

    def slots_of(k):
        return (2 * k - 1, 2 * k)

    def receive(ch, k, sends):
        for sec in range(2):
            for h in range(2):
                for way in range(2):
                    if sends == 0 and way != sec:
                        continue
                    ring(ch, way, sec, k, h).wait_recv()
                    if sends == 2 or (sends == 1 and way == sec):
                        ring(ch, way, sec, k + 1, h).start()

    def sent(ch, k, far=False):
        for sec in range(2):
            for h in range(2):
                for way in range(2):
                    if not far or way == sec:
                        ring(ch, way, sec, k, h).wait_send()

    def when(condition, action):
        if isinstance(condition, bool):
            if condition:
                action()
        else:
            pl.when(condition)(action)

    def mirror_piece(f):
        hid_send(f).wait()
        sib_send(f).start()
        when(f + DEPTH < pieces, lambda: hid_send(f + DEPTH).start())

    def turn_piece(f):
        sib_send(f).wait()
        for ex in range(2):
            turn(1, ex, f, hid_mir)

    for h in range(2):
        mir_first[h].wait()
        for way in range(2):
            ring(0, way, 1, 1, h).start()
    mir_second.start()
    for f in range(min(DEPTH, pieces)):
        hid_send(f).start()
    build((0,))
    pick(0, (0,))
    pair_copy(0, 0, 0, 1).start()

    pairs = half // 2
    lead = pairs // 2

    def early(j, h):
        sec, k = j % 2 if isinstance(j, int) else lax.rem(j, 2), j // 2 + 1
        if isinstance(j, int):
            if k >= 2:
                for way in range(2):
                    ring(1, way, sec, k - 1, h).wait_recv()
        else:

            @pl.when(k >= 2)
            def _():
                for way in range(2):
                    ring(1, way, sec, k - 1, h).wait_recv()

        for way in range(2):
            ring(1, way, sec, k, h).start()

    def steps(ch, j, last):
        k = 2 * j + 1
        if ch == 0:
            receive(ch, k, 1 if last else 2)
            when(j == 1, lambda: mir_second.wait())
            early(j, 0)
        elif isinstance(j, int):
            if k >= lead:
                receive(ch, k, 1 if last else 2)
        else:
            when(k >= lead, lambda: receive(ch, k, 1 if last else 2))
        if ch == 0:
            build(slots_of(k))
        pick(ch, slots_of(k))
        pair_copy(ch, k, slots_of(k)[0], 2).start()
        when(k >= 3, lambda: merge(ch, k - 2, slots_of(k - 2)))
        if ch == 0:
            when(j >= 2, lambda: turn_piece(j - 2))
            turn_own(2 * j)
        else:
            piece = pairs - 1 + 2 * j
            when(piece - 1 < pieces, lambda: turn_piece(piece - 1))
            when(piece < pieces, lambda: mirror_piece(piece))

            def rest_of_first():
                merge(0, half - 1, slots_of(half - 1))
                merge(0, half, (2 * half - 1,))

            when(j == 0, rest_of_first)
            more = (3 * j - 1 < pieces) if isinstance(j, int) else (j >= 1) & (3 * j - 1 < pieces)
            if not isinstance(j, int) or j >= 1:
                when(more, lambda: send_first(3 * j - 1))
            if last:
                lax.fori_loop(0, pieces // 2, begin, 0)
        sent(ch, k)

        k = k + 1
        receive(ch, k, 0 if last else 2)
        if ch == 0:
            early(j, 1)
        at = (2 * half - 1,) if last else slots_of(k)
        if ch == 0:
            build(at)
        pick(ch, at)
        pair_copy(ch, k, at[0], len(at)).start()
        when(j == 0, lambda: merge(ch, 0, (0,)))
        when(j >= 1, lambda: merge(ch, k - 2, slots_of(k - 2)))
        if ch == 0:
            when(j >= 1, lambda: mirror_piece(j - 1))
            turn_own(2 * j + 1)
        else:
            when(piece < pieces, lambda: turn_piece(piece))
            when(piece + 1 < pieces, lambda: mirror_piece(piece + 1))
            when(3 * j < pieces, lambda: send_first(3 * j))
            when(3 * j + 1 < pieces, lambda: send_first(3 * j + 1))
        sent(ch, k, far=last)

    def whole(ch):
        if pairs > 1:

            def body(j, carry):
                steps(ch, j, False)
                return carry

            lax.fori_loop(0, pairs - 1, body, 0)
        steps(ch, pairs - 1, True)

    whole(0)
    pick(1, (0,))
    pair_copy(1, 0, 0, 1).start()

    whole(1)
    merge(1, half - 1, slots_of(half - 1))
    merge(1, half, (2 * half - 1,))

    def out_copy(f):
        at = pl.ds(pl.multiple_of(f * wide, wide), wide)
        return pltpu.make_async_copy(
            out_b.at[f], out_ref.at[pair_index, :, :, at], out_l.at[f]
        )

    def finish(f, carry):
        at = pl.ds(pl.multiple_of(f * wide, wide), wide)
        for ex in range(2):
            late = total[ex, at, :] + product(1, ex, at, slice(early_rows, blocks * rows))
            out_b[f, ex] = (late * factor).astype(BF).T
        out_copy(f).start()
        return carry

    lax.fori_loop(0, pieces // 2, finish, 0)

    def close(f, carry):
        lat_send(f).wait()
        return carry

    lax.fori_loop(0, pieces, close, 0)

    def close_own(f, carry):
        out_copy(f).wait()
        return carry

    lax.fori_loop(0, pieces // 2, close_own, 0)


def move(parts, src, dst, held, come, go):
    size = src.shape[2] // parts
    places = [
        (p, ex, pl.ds(i * size, size)) for p in range(2) for ex in range(2) for i in range(parts)
    ]
    reads = [
        pltpu.make_async_copy(src.at[at], held.at[at], come.at[i]) for i, at in enumerate(places)
    ]
    writes = [
        pltpu.make_async_copy(held.at[at], dst.at[at], go.at[i]) for i, at in enumerate(places)
    ]
    for read in reads:
        read.start()
    for read, write in zip(reads, writes):
        read.wait()
        write.start()
    for write in writes:
        write.wait()


def local(routes, weights, cotangent, hidden):
    tokens = routes.shape[1]
    tops = routes.shape[2]
    slot_count, units = hidden.shape[2], hidden.shape[3]
    n_exp = lax.axis_size("expert")
    sections = lax.axis_size("section")
    cap = slot_count // n_exp
    rows = 2 * cap
    half = n_exp // 4
    blocks = 2 * half
    width = cotangent.shape[2] // sections
    pieces = units // LANE
    cfg = (half, cap, width, pieces, tops)
    hbm = pl.BlockSpec(memory_space=pl.ANY)
    dma = pltpu.SemaphoreType.DMA
    grad = pl.pallas_call(
        functools.partial(kernel, cfg),
        out_shape=jax.ShapeDtypeStruct((2, 2, width, units), BF),
        in_specs=[hbm, hbm, hbm, hbm],
        out_specs=hbm,
        scratch_shapes=[
            pltpu.VMEM((tops, tokens), jnp.int32),
            pltpu.VMEM((tops, tokens), F32),
            pltpu.VMEM((tokens, sections * width), BF),
            dma((3,)),
            pltpu.VMEM((sections * width, tokens), BF),
            pltpu.VMEM((2, blocks, width + 4 * tops, tokens), BF),
            pltpu.VMEM((2, blocks, width, tokens), BF),
            pltpu.VMEM((2, width + 4 * tops, tokens), BF),
            pltpu.VMEM((2, pieces, slot_count, LANE), BF),
            pltpu.VMEM((2, pieces, slot_count, LANE), BF),
            pltpu.VMEM((2, 2, units, slot_count), BF),
            pltpu.VMEM((tokens, tokens), BF),
            pltpu.VMEM((2, blocks, 2 * rows, tokens), BF),
            pltpu.VMEM((2, blocks, 2 * rows, tokens), F32),
            pltpu.VMEM((2, 2, blocks, 2, rows, width), BF),
            pltpu.VMEM((2, blocks, 2, rows, width), BF),
            pltpu.VMEM((2, 2, 2, slot_count, width), BF),
            pltpu.VMEM((pieces, 2, width, LANE), BF),
            pltpu.VMEM((pieces // 2, 2, width, 2 * LANE), BF),
            pltpu.VMEM((2, units, width), F32),
            dma((2, 2, 2, half + 1, 2)),
            dma((2, 2, 2, half + 1, 2)),
            dma((3,)),
            dma((3,)),
            dma((2, pieces)),
            dma((pieces,)),
            dma((pieces,)),
            dma((pieces,)),
            dma((pieces,)),
            dma((2, half + 1)),
            dma((2, half + 1)),
            dma((pieces,)),
            dma((pieces,)),
            dma((pieces // 2,)),
        ],
        compiler_params=pltpu.CompilerParams(
            collective_id=0, has_side_effects=True, vmem_limit_bytes=63 * 1024 * 1024
        ),
        cost_estimate=pl.CostEstimate(
            flops=8 * units * slot_count * width * 4, bytes_accessed=8 << 20, transcendentals=0
        ),
    )(
        jnp.swapaxes(routes, 1, 2)[0],
        jnp.swapaxes(weights, 1, 2)[0],
        cotangent[0],
        hidden[0],
    )
    grad = pl.pallas_call(
        functools.partial(move, 2),
        out_shape=jax.ShapeDtypeStruct(grad.shape, grad.dtype),
        in_specs=[hbm],
        out_specs=hbm,
        scratch_shapes=[pltpu.VMEM(grad.shape, grad.dtype), dma((8,)), dma((8,))],
        compiler_params=pltpu.CompilerParams(vmem_limit_bytes=63 * 1024 * 1024),
    )(grad)
    return jnp.swapaxes(grad, 2, 3)


def solution(mesh):
    return jax.shard_map(
        local,
        mesh=mesh,
        in_specs=(
            P("section", "expert", None),
            P("section", "expert", None),
            P("section", "expert", "dp"),
            P("section", "expert", None, None),
        ),
        out_specs=P(None, "expert", None, ("dp", "section")),
        check_vma=False,
    )
```
